1024 devices in a mesh: dp: 32 (over z_lo, x), expert: 8 (over z_hi, core), tensor: 4 (over y).
Axes of the slice: x: 4, y: 4, z: 32 (z_hi: 4, z_lo: 8; z = z_hi * 8 + z_lo), core: 2. Of those that a mesh axis runs over, the one named last changes fastest.
Arguments:
- residual: bfloat16 [32768, 3072], P(('dp', 'expert'), 'tensor'), parts along dimension 0, may hold values from -40 to 40
- expert_ids: int32 [32768, 4], P(('dp', 'expert')), parts along dimension 0, may hold values from 0 to 15, all different within a row; in each aligned block of 128 rows (0 to 127, 128 to 255, ...) at most 40 rows name the same one
- gate_prob: float32 [32768, 4], P(('dp', 'expert')), parts along dimension 0, may hold values from 0.05 to 1
- expert_hidden: bfloat16 [8, 256, 40, 5632], P('expert', 'dp', None, 'tensor'), parts along dimension 1, may hold values from -6 to 6
- w_down: bfloat16 [8, 5632, 3072], P('expert', 'tensor'), may hold values from -0.078125 to 0.078125
- norm_gain: float32 [3072], P('tensor'), may hold values from 0.1 to 1.9
Outputs:
- normed: bfloat16 [32768, 3072], P(('dp', 'expert'), 'tensor'), parts along dimension 0
The draws below stay inside these ranges and needn't reach their ends.
There are 32 independent parts, one for each index of `dp`. The reference program is written for one: setup_inputs(seed, part) draws one part's arguments, and reference() takes and returns one part's arrays. A program takes and returns all parts, laid end to end along the dimension named above; an argument that names none is the same for every part. Nothing has to cross between parts.
Inputs may be any that keep to these rules, and one draw needn't show every extreme that they name: `expert_ids`: each row names 4 different experts. Within the 128 rows of one index of expert, no expert is named more than 40 times, a bound that some block reaches in some of them.
All inputs are finite; a program needn't handle non-finite values.
Results may differ from the reference program's by a relative error of at most 0.008.
Values may be sent and summed in bfloat16 or wider, within the bound.
No kernel may reach another device: no remote copies, remote signals or barrier semaphores. Data moves between devices by JAX's collectives and lax.ppermute only.
A program may use at most 64 MiB of HBM per device.

```python
import math
import jax
import jax.numpy as jnp
import numpy as np
from jax import lax

D = 3072
FF = 5632
EXPERTS = 16
TOPK = 4
TOK_DEV = 128
CAP = 40
FLIGHT = 8
GROUPS = 4
TOKENS = 1024


def draw_residual(key, part):
    key = jax.random.fold_in(key, 11)
    key_base, key_column, key_row = jax.random.split(key, 3)
    column = jnp.arange(D, dtype=jnp.float32) / D
    column_scale = 0.5 * jnp.power(3.0, column) * jnp.exp(jax.random.uniform(key_column, (D,), jnp.float32, -0.6, 0.6))
    base = jnp.clip(jax.random.normal(key_base, (TOKENS, D), jnp.float32), -4.0, 4.0)
    row_scale = jnp.exp(jax.random.uniform(key_row, (TOKENS, 1), jnp.float32, -1.15, 1.15))
    return (base * row_scale * column_scale[None, :]).astype(jnp.bfloat16)


def block_levels(key, shape, shards, least, high):
    factor_of, own = 1.0, jax.random.fold_in(key, 6)
    for position, blocks in shards:
        draws = jnp.exp(jax.random.uniform(jax.random.fold_in(own, position), (blocks,), jnp.float32, least / len(shards), high / len(shards)))
        factor_of = factor_of * jnp.repeat(draws, shape[position] // blocks).reshape([-1 if axis == position else 1 for axis in range(len(shape))])
    return factor_of


def routed_block(stream_key, own, number, rows, amount, top, most, slope):
    sequence = jax.random.permutation(stream_key, amount)
    crowded, ordinary = shares(amount, rows * top, most, slope, True), shares(amount, rows * top, most, slope, False)
    places = jnp.arange(amount)

    def named(tallies, offset_by):
        used = int((tallies > 0).sum())
        fixed = max(1, used // 4)
        moved = fixed + (places - fixed + offset_by * (used - fixed)) % max(1, amount - fixed)
        return jnp.zeros((amount,), jnp.int32).at[sequence[jnp.where(places < fixed, places, moved)]].set(jnp.asarray(tallies, jnp.int32))

    tallies = jnp.where(number % 4 == 0, named(crowded, number // 4), named(ordinary, number - number // 4 - 1))
    mixed = jax.random.permutation(jax.random.fold_in(own, 3), amount)
    source_of, sink = mixed[0:amount // 2 * 2:2], mixed[1:amount // 2 * 2:2]
    room = jnp.minimum(tallies[source_of] - 1, most - tallies[sink]) // 2
    room = jnp.where((source_of == sequence[0]) | (sink == sequence[0]) | (tallies[sink] == 0), 0, jnp.maximum(room, 0))
    moved = jax.random.randint(jax.random.fold_in(own, 4), (amount // 2,), 0, 1 << 20) % (room + 1)
    tallies = tallies.at[source_of].add(-moved).at[sink].add(moved)
    labels = jnp.searchsorted(jnp.cumsum(tallies), jnp.arange(rows * top), side="right").astype(jnp.int32)
    grid = labels.reshape(top, rows).T
    grid = grid[jax.random.permutation(jax.random.fold_in(own, 1), rows)]
    offset_by = jax.random.randint(jax.random.fold_in(own, 2), (rows, 1), 0, top)
    return jnp.take_along_axis(grid, (jnp.arange(top)[None, :] + offset_by) % top, axis=1)


def shares(number_of, total, bound, skew, full):
    portions = [(1 << 20) // math.isqrt(standing ** skew) + 1 for standing in range(1, number_of + 1)]
    largest = bound if full else min(bound, max(-(-total // number_of), total * portions[0] // sum(portions)))
    least = 1 if total - largest >= number_of - 1 else 0
    given, spare = [largest] + [least] * (number_of - 1), total - largest - least * (number_of - 1)
    while spare > 0:
        free = [i for i in range(1, number_of) if given[i] < largest] or [i for i in range(1, number_of) if given[i] < bound]
        whole, left = sum([portions[i] for i in free]), spare
        for i in free:
            addition = min(bound - given[i], max(1, left * portions[i] // whole), spare)
            given[i] = given[i] + addition
            spare = spare - addition
    return np.array(given)


def noise(stream_key, extent, spread, limit, shards=(), held_as=jnp.bfloat16):
    drawn = jax.random.normal(stream_key, extent, jnp.float32) * spread
    if len(shards) > 0:
        drawn = block_levels(stream_key, extent, shards, -0.22, 0.18) * drawn
    return jnp.clip(drawn, min=-limit, max=limit).astype(held_as)


def setup_inputs(seed: int = 0, part: int = 0) -> dict:
    seeds = jax.random.split(jax.random.key(seed), 7)
    own_keys = jax.random.split(jax.random.fold_in(seeds[6], part), 7)
    residual = draw_residual(jax.random.fold_in(jax.random.fold_in(seeds[6], part), 71), part)
    expert_ids_keys = jax.random.split(jax.random.fold_in(own_keys[1], 1), TOKENS // TOK_DEV)
    expert_ids_turns = jax.random.permutation(jax.random.fold_in(own_keys[1], 3), TOKENS // TOK_DEV)
    expert_ids = jax.vmap(lambda own, number: routed_block(jax.random.fold_in(own_keys[1], 2), own, number, TOK_DEV, EXPERTS, TOPK, CAP, 2))(expert_ids_keys, expert_ids_turns).reshape((TOKENS, TOPK))
    gate_prob = jnp.clip(jnp.exp(math.log(1.0) - 2.9957323 * jax.random.uniform(own_keys[2], (TOKENS, TOPK), jnp.float32) ** block_levels(own_keys[2], (TOKENS, TOPK), ((0, 8),), -0.2, 0.2)), 0.05, 1.0)
    expert_hidden = noise(own_keys[3], (FLIGHT, FLIGHT, CAP, FF), 1.0, 6.0, ((0, 8), (3, 4)))
    w_down = noise(seeds[4], (FLIGHT, FF, D), FF ** -0.5, 0.078125, ((0, 8), (1, 4)))
    norm_gain = jnp.clip(1.0 + 0.18 * jax.random.normal(seeds[5], (D,), jnp.float32), 0.1, 1.9)
    return dict(residual=residual, expert_ids=expert_ids, gate_prob=gate_prob, expert_hidden=expert_hidden, w_down=w_down, norm_gain=norm_gain)


def slot_positions(expert_ids):
    onehot = (expert_ids[..., None] == jnp.arange(EXPERTS, dtype=jnp.int32)).astype(jnp.int32)
    named_count = lax.optimization_barrier(jnp.sum(onehot, axis=-2))
    prefix = jnp.cumsum(named_count, axis=-2) - named_count
    return jnp.take_along_axis(prefix, expert_ids, axis=-1).astype(jnp.int32)

def reference(residual, expert_ids, gate_prob, expert_hidden, w_down, norm_gain):
    blocks = expert_ids.reshape(FLIGHT, TOK_DEV, TOPK)
    positions = slot_positions(blocks)
    source = jnp.arange(FLIGHT, dtype=jnp.int32)[:, None, None]
    in_window = blocks < FLIGHT
    flat_index = jnp.where(in_window, blocks * (FLIGHT * CAP) + source * CAP + positions, 0)
    flat_index = flat_index.reshape(TOKENS, TOPK).astype(jnp.int32)
    weight = jnp.where(in_window.reshape(TOKENS, TOPK), gate_prob, jnp.float32(0.0))
    width = FF // GROUPS

    def one_expert(pair):
        hidden, down = pair
        hidden = hidden.reshape(FLIGHT * CAP, FF)
        running = jnp.zeros((FLIGHT * CAP, D), jnp.float32)
        for group_index in range(GROUPS):
            lower = group_index * width
            partial_value = jnp.dot(hidden[:, lower:lower + width], down[lower:lower + width], preferred_element_type=jnp.float32).astype(jnp.bfloat16)
            partial_value = lax.optimization_barrier(partial_value)
            running = running + partial_value.astype(jnp.float32)
        return running
    expert_rows = lax.map(one_expert, (expert_hidden, w_down)).reshape(FLIGHT * FLIGHT * CAP, D)
    picked = jnp.take(expert_rows, flat_index, axis=0)
    moe = lax.optimization_barrier(jnp.sum(picked * weight[..., None], axis=1))
    stream = moe + residual.astype(jnp.float32)
    inverse_rms = lax.rsqrt(lax.optimization_barrier(jnp.mean(stream * stream, axis=1, keepdims=True)) + 1e-05)
    return (stream * inverse_rms * norm_gain.astype(jnp.float32)).astype(jnp.bfloat16)
```

```python
import functools

import jax
import jax.numpy as jnp
from jax import lax
from jax.experimental import pallas as pl
from jax.experimental.pallas import tpu as pltpu
from jax.sharding import Mesh
from jax.sharding import PartitionSpec as P

EXPERTS = 16
KEY_STRIDE = 64
EPSILON = 1e-05
VMEM_LIMIT = 32 * 1024 * 1024
DOWN_VMEM_LIMIT = 48 * 1024 * 1024
CORES = 2
FIRST_FLOPS = 40_000_000_000
W_BLOCK = 256
PARTS = ((2,), (1, 3, 0))


def kernel_params(limit=VMEM_LIMIT):
    return pltpu.CompilerParams(vmem_limit_bytes=limit)


def routing_kernel(ids_ref, gate_ref, *refs):
    tables = len(refs) // 3
    tokens, topk = ids_ref.shape
    ids = ids_ref[...]
    gate = gate_ref[...]
    lane = lax.broadcasted_iota(jnp.int32, (tokens, EXPERTS), 1)
    hits = [ids[:, k : k + 1] == lane for k in range(topk)]
    named = functools.reduce(jnp.add, [jnp.where(h, 1.0, 0.0) for h in hits])
    earlier = jnp.where(
        lax.broadcasted_iota(jnp.int32, (tokens, tokens), 1)
        < lax.broadcasted_iota(jnp.int32, (tokens, tokens), 0),
        1.0,
        0.0,
    )
    prefix = jnp.dot(
        earlier.astype(jnp.bfloat16),
        named.astype(jnp.bfloat16),
        preferred_element_type=jnp.float32,
    )
    positions = [
        jnp.sum(jnp.where(hits[k], prefix, 0.0), axis=1, keepdims=True) for k in range(topk)
    ]
    keys = [
        ids[:, k : k + 1] * KEY_STRIDE + positions[k].astype(jnp.int32) for k in range(topk)
    ]
    for key_ref, high_ref, low_ref in zip(refs[:tables], refs[tables::2], refs[tables + 1 :: 2]):
        key_of_slot = key_ref[...]
        table = jnp.zeros((tokens, key_ref.shape[1]), jnp.float32)
        for k in range(topk):
            table = table + jnp.where(keys[k] == key_of_slot, gate[:, k : k + 1], 0.0)
        high = table.astype(jnp.bfloat16)
        high_ref[...] = high
        low_ref[...] = (table - high.astype(jnp.float32)).astype(jnp.bfloat16)


def routing_tables(ids, gate, keys):
    out = pl.pallas_call(
        routing_kernel,
        out_shape=[
            jax.ShapeDtypeStruct((ids.shape[0], key.shape[1]), jnp.bfloat16)
            for key in keys
            for _ in range(2)
        ],
        compiler_params=kernel_params(),
        name="routing_tables",
    )(ids, gate, *keys)
    return list(zip(out[0::2], out[1::2]))


def down_kernel(parts, place_ref, hidden_ref, w_ref, *refs):
    out_refs, refs = refs[: len(parts)], refs[len(parts) :]
    held_refs, (rows_ref, w_held, rows_sem, w_sem, out_sem) = refs[: len(parts)], refs[len(parts) :]
    chips, height, depth = hidden_ref.shape
    blocks, _, width = w_held.shape
    _, groups, _, capacity, quarter = out_refs[0].shape
    per_group = quarter // width
    shifts = [s for part in parts for s in part]
    row_copies = [
        pltpu.make_async_copy(
            hidden_ref.at[lax.rem(place_ref[0] + s, chips)], rows_ref.at[i], rows_sem.at[i]
        )
        for i, s in enumerate(shifts)
    ]

    def w_copy(n):
        columns = pl.ds(pl.multiple_of(n * width, width), width)
        return pltpu.make_async_copy(w_ref.at[:, columns], w_held.at[n], w_sem.at[n])

    def out_copies(g):
        return [
            pltpu.make_async_copy(held.at[:, g], out.at[:, g], out_sem.at[i, g])
            for i, (held, out) in enumerate(zip(held_refs, out_refs))
        ]

    for copy in row_copies:
        copy.start()

    @pl.loop(0, blocks)
    def _(n):
        w_copy(n).start()

    for copy in row_copies:
        copy.wait()
    rows = rows_ref[...].reshape(len(shifts) * height, depth)

    @pl.loop(0, groups)
    def _(g):
        @pl.loop(0, per_group)
        def _(j):
            n = g * per_group + j
            w_copy(n).wait()
            value = jnp.dot(rows, w_held[n], preferred_element_type=jnp.float32)
            columns = pl.ds(pl.multiple_of(j * width, width), width)
            first = 0
            for part, held in zip(parts, held_refs):
                for i in range(len(part)):
                    for core in range(CORES):
                        piece = value[first : first + capacity]
                        held[core, g, i, :, columns] = piece.astype(jnp.bfloat16)
                        first += capacity

        for copy in out_copies(g):
            copy.start()

    @pl.loop(0, groups)
    def _(g):
        for copy in out_copies(g):
            copy.wait()


def down(place, hidden, weights, parts, groups):
    chips, height, depth = hidden.shape
    width = W_BLOCK
    quarter = weights.shape[1] // groups
    capacity = height // CORES
    blocks = weights.shape[1] // width
    shapes = [(CORES, groups, len(part), capacity, quarter) for part in parts]
    rows = sum(map(len, parts)) * height
    anywhere = pl.BlockSpec(memory_space=pl.ANY)
    return pl.pallas_call(
        functools.partial(down_kernel, parts),
        in_specs=[pl.BlockSpec(memory_space=pltpu.SMEM), anywhere, anywhere],
        out_specs=[anywhere] * len(parts),
        out_shape=[jax.ShapeDtypeStruct(shape, jnp.bfloat16) for shape in shapes],
        scratch_shapes=[pltpu.VMEM(shape, jnp.bfloat16) for shape in shapes]
        + [
            pltpu.VMEM((sum(map(len, parts)), height, depth), jnp.bfloat16),
            pltpu.VMEM((blocks, depth, width), jnp.bfloat16),
            pltpu.SemaphoreType.DMA((sum(map(len, parts)),)),
            pltpu.SemaphoreType.DMA((blocks,)),
            pltpu.SemaphoreType.DMA((len(parts), groups)),
        ],
        compiler_params=kernel_params(DOWN_VMEM_LIMIT),
        cost_estimate=pl.CostEstimate(
            flops=2 * rows * depth * quarter * groups,
            bytes_accessed=2 * (weights.size + rows * depth + rows * quarter * groups),
            transcendentals=0,
        ),
        name="down_rows",
    )(place, hidden, weights)


def add_kernel(count, later, part_ref, *refs):
    out_refs = refs[later : later + count]
    groups = part_ref.shape[1]
    for i, out_ref in enumerate(out_refs):
        for core in range(CORES):
            values = [part_ref[core, g, i].astype(jnp.float32) for g in range(groups)]
            out_ref[core] = functools.reduce(jnp.add, values).astype(jnp.bfloat16)


def add_groups(parts, later):
    cores, groups, count, capacity, quarter = parts.shape
    anywhere = pl.BlockSpec(memory_space=pl.ANY)
    whole = pl.BlockSpec(memory_space=pltpu.VMEM)
    out = pl.pallas_call(
        functools.partial(add_kernel, count, len(later)),
        in_specs=[whole] + [anywhere] * len(later),
        out_specs=[whole] * count + [anywhere] * len(later),
        out_shape=[jax.ShapeDtypeStruct((cores, capacity, quarter), jnp.bfloat16)] * count
        + [jax.ShapeDtypeStruct(v.shape, v.dtype) for v in later],
        input_output_aliases={1 + i: count + i for i in range(len(later))},
        compiler_params=kernel_params(),
        cost_estimate=pl.CostEstimate(
            flops=parts.size, bytes_accessed=3 * parts.size, transcendentals=0
        ),
        name="add_groups",
    )(parts, *later)
    return out[:count], out[count:]


def picked(table, piece_refs):
    rows = jnp.concatenate(
        [r[core].astype(jnp.float32) for r in piece_refs for core in range(CORES)], axis=0
    )
    rows = rows.astype(jnp.bfloat16)
    high_ref, low_ref = table
    return jnp.dot(high_ref[...], rows, preferred_element_type=jnp.float32) + jnp.dot(
        low_ref[...], rows, preferred_element_type=jnp.float32
    )


def combine_first_kernel(high_ref, low_ref, residual_ref, *refs):
    refs[-1][...] = picked((high_ref, low_ref), refs[:-1]) + residual_ref[...].astype(jnp.float32)


def combine_first(table, residual, pieces):
    return pl.pallas_call(
        combine_first_kernel,
        out_shape=jax.ShapeDtypeStruct(residual.shape, jnp.float32),
        compiler_params=kernel_params(),
        cost_estimate=pl.CostEstimate(
            flops=FIRST_FLOPS, bytes_accessed=8 * residual.size, transcendentals=0
        ),
        name="combine_first",
    )(*table, residual, *pieces)


def combine_last_kernel(high_ref, low_ref, begun_ref, *refs):
    piece_refs, (stream_ref, square_ref) = refs[:-2], refs[-2:]
    stream = begun_ref[...] + picked((high_ref, low_ref), piece_refs)
    stream_ref[...] = stream
    square = stream * stream
    lanes = stream.shape[0]
    folded = functools.reduce(
        jnp.add, [square[:, i : i + lanes] for i in range(0, square.shape[1], lanes)]
    )
    square_ref[...] = jnp.sum(folded.T, axis=0, keepdims=True)


def combine_last(table, begun, pieces):
    return pl.pallas_call(
        combine_last_kernel,
        out_shape=(
            jax.ShapeDtypeStruct(begun.shape, jnp.float32),
            jax.ShapeDtypeStruct((1, begun.shape[0]), jnp.float32),
        ),
        compiler_params=kernel_params(),
        name="combine_last",
    )(*table, begun, *pieces)


def norm_kernel(width, stream_ref, square_ref, gain_ref, out_ref):
    lanes = stream_ref.shape[0]
    inverse = lax.rsqrt(square_ref[...] / width + EPSILON)
    inverse = jnp.broadcast_to(inverse, (lanes, lanes)).T
    for i in range(0, stream_ref.shape[1], lanes):
        out_ref[:, i : i + lanes] = (
            stream_ref[:, i : i + lanes] * inverse * gain_ref[:, i : i + lanes]
        ).astype(jnp.bfloat16)


def norm(stream, square_total, gain, width):
    return pl.pallas_call(
        functools.partial(norm_kernel, width),
        out_shape=jax.ShapeDtypeStruct(stream.shape, jnp.bfloat16),
        compiler_params=kernel_params(),
        name="norm",
    )(stream, square_total, gain)


def body(residual, expert_ids, gate_prob, expert_hidden, w_down, norm_gain):
    chips = lax.axis_size("chip")
    groups = lax.axis_size("tensor")
    capacity, depth = expert_hidden.shape[2:]
    model_width = w_down.shape[2]
    chip = lax.axis_index("chip")
    place = jnp.stack([chip]).astype(jnp.int32)

    def to_chip(value, shift):
        if shift == 0:
            return value
        return lax.ppermute(value, "chip", [(i, (i + shift) % chips) for i in range(chips)])

    def keys_of(shifts):
        expert = jnp.stack(
            [(chip + chips - s) % chips * CORES + core for s in shifts for core in range(CORES)]
        )
        slot = jnp.arange(capacity, dtype=jnp.int32)
        return (expert[:, None] * KEY_STRIDE + slot[None, :]).reshape(1, -1)

    first, last = (2, 0), (1, 3)
    table_first, table_last = routing_tables(
        expert_ids, gate_prob, [keys_of(first), keys_of(last)]
    )

    hidden = expert_hidden.reshape(chips, CORES * capacity, depth)
    values = down(place, hidden, w_down[0], PARTS, groups)
    pieces = {}
    for part in PARTS:
        value, *values = values
        shape = value.shape
        value = lax.all_to_all(
            value.reshape(CORES * groups, *shape[2:]), ("core", "tensor"), 0, 0, tiled=True
        )
        summed, values = add_groups(value.reshape(shape), values)
        pieces.update((s, to_chip(v, s)) for v, s in zip(summed, part))
    begun = combine_first(table_first, residual, [pieces[s] for s in first])
    stream, squares = combine_last(table_last, begun, [pieces[s] for s in last])
    square_total = lax.psum(squares, "tensor")
    return norm(stream, square_total, norm_gain[None, :], model_width)


def solution(mesh):
    dp, expert, tensor = mesh.devices.shape
    cores = Mesh(
        mesh.devices.reshape(dp, expert // CORES, CORES, tensor), ("dp", "chip", "core", "tensor")
    )
    tokens = ("dp", "chip", "core")
    placed = (
        P(tokens, "tensor"),
        P(tokens, None),
        P(tokens, None),
        P(("chip", "core"), "dp", None, "tensor"),
        P(("chip", "core"), "tensor", None),
        P("tensor"),
    )
    return jax.shard_map(
        body, mesh=cores, in_specs=placed, out_specs=P(tokens, "tensor"), check_vma=False
    )
```

```python
import functools

import jax
import jax.numpy as jnp
from jax import lax
from jax.experimental import pallas as pl
from jax.experimental.pallas import tpu as pltpu
from jax.sharding import Mesh
from jax.sharding import PartitionSpec as P

EXPERTS = 16
KEY_STRIDE = 64
EPSILON = 1e-05
VMEM_LIMIT = 32 * 1024 * 1024
DOWN_VMEM_LIMIT = 60 * 1024 * 1024
HERE_VMEM_LIMIT = 48 * 1024 * 1024
CORES = 2
FIRST_FLOPS = 40_000_000_000
W_BLOCK = 512
AHEAD = 3
PARTS = ((2,), (3, 1), (0,))


def kernel_params(limit=VMEM_LIMIT):
    return pltpu.CompilerParams(vmem_limit_bytes=limit)


def routing_kernel(ids_ref, gate_ref, *refs):
    tables = len(refs) // 3
    tokens, topk = ids_ref.shape
    ids = ids_ref[...]
    gate = gate_ref[...]
    lane = lax.broadcasted_iota(jnp.int32, (tokens, EXPERTS), 1)
    hits = [ids[:, k : k + 1] == lane for k in range(topk)]
    named = functools.reduce(jnp.add, [jnp.where(h, 1.0, 0.0) for h in hits])
    earlier = jnp.where(
        lax.broadcasted_iota(jnp.int32, (tokens, tokens), 1)
        < lax.broadcasted_iota(jnp.int32, (tokens, tokens), 0),
        1.0,
        0.0,
    )
    prefix = jnp.dot(
        earlier.astype(jnp.bfloat16),
        named.astype(jnp.bfloat16),
        preferred_element_type=jnp.float32,
    )
    positions = [
        jnp.sum(jnp.where(hits[k], prefix, 0.0), axis=1, keepdims=True) for k in range(topk)
    ]
    keys = [
        ids[:, k : k + 1] * KEY_STRIDE + positions[k].astype(jnp.int32) for k in range(topk)
    ]
    for key_ref, high_ref, low_ref in zip(refs[:tables], refs[tables::2], refs[tables + 1 :: 2]):
        key_of_slot = key_ref[...]
        table = jnp.zeros((tokens, key_ref.shape[1]), jnp.float32)
        for k in range(topk):
            table = table + jnp.where(keys[k] == key_of_slot, gate[:, k : k + 1], 0.0)
        high = table.astype(jnp.bfloat16)
        high_ref[...] = high
        low_ref[...] = (table - high.astype(jnp.float32)).astype(jnp.bfloat16)


def routing_tables(ids, gate, keys):
    out = pl.pallas_call(
        routing_kernel,
        out_shape=[
            jax.ShapeDtypeStruct((ids.shape[0], key.shape[1]), jnp.bfloat16)
            for key in keys
            for _ in range(2)
        ],
        compiler_params=kernel_params(),
        name="routing_tables",
    )(ids, gate, *keys)
    return list(zip(out[0::2], out[1::2]))


def down_kernel(parts, place_ref, hidden_ref, w_ref, *refs):
    refs = refs[len(refs) - 2 * len(parts) - 5 :]
    out_refs, refs = refs[: len(parts)], refs[len(parts) :]
    held_refs, (rows_ref, w_held, rows_sem, w_sem, out_sem) = refs[: len(parts)], refs[len(parts) :]
    chips, height, _ = hidden_ref.shape
    blocks, _, width = w_held.shape
    _, groups, _, capacity, quarter = out_refs[0].shape
    shifts = [s for part in parts for s in part]
    row_copies = [
        pltpu.make_async_copy(
            hidden_ref.at[jnp.bitwise_xor(place_ref[0], s)],
            rows_ref.at[i * height : (i + 1) * height],
            rows_sem.at[i],
        )
        for i, s in enumerate(shifts)
    ]
    w_copies = [
        pltpu.make_async_copy(
            w_ref.at[:, n * width : (n + 1) * width], w_held.at[n], w_sem.at[n]
        )
        for n in range(blocks)
    ]
    out_copies = [
        [
            pltpu.make_async_copy(held.at[:, g], out.at[:, g], out_sem.at[i, g])
            for i, (held, out) in enumerate(zip(held_refs, out_refs))
        ]
        for g in range(groups)
    ]
    for copy in row_copies + w_copies[:AHEAD]:
        copy.start()
    for copy in row_copies:
        copy.wait()
    stored = 0
    for n in range(blocks):
        w_copies[n].wait()
        if n + AHEAD < blocks:
            w_copies[n + AHEAD].start()
        value = jnp.dot(rows_ref[...], w_held[n], preferred_element_type=jnp.float32)
        begin, end = n * width, (n + 1) * width
        left = begin
        while left < end:
            g = left // quarter
            right = min(end, (g + 1) * quarter)
            first = 0
            for part, held in zip(parts, held_refs):
                for i in range(len(part)):
                    for core in range(CORES):
                        held[core, g, i, :, left - g * quarter : right - g * quarter] = value[
                            first : first + capacity, left - begin : right - begin
                        ].astype(jnp.bfloat16)
                        first += capacity
            left = right
        while (stored + 1) * quarter <= end:
            for copy in out_copies[stored]:
                copy.start()
            stored += 1
    for copies in out_copies:
        for copy in copies:
            copy.wait()


def down(place, hidden, weights, parts, groups, limit, after=()):
    chips, height, depth = hidden.shape
    width = W_BLOCK
    quarter = weights.shape[1] // groups
    capacity = height // CORES
    blocks = weights.shape[1] // width
    shapes = [(CORES, groups, len(part), capacity, quarter) for part in parts]
    count = sum(map(len, parts))
    rows = count * height
    anywhere = pl.BlockSpec(memory_space=pl.ANY)
    return pl.pallas_call(
        functools.partial(down_kernel, parts),
        in_specs=[pl.BlockSpec(memory_space=pltpu.SMEM)] + [anywhere] * (2 + len(after)),
        out_specs=[anywhere] * len(parts),
        out_shape=[jax.ShapeDtypeStruct(shape, jnp.bfloat16) for shape in shapes],
        scratch_shapes=[pltpu.VMEM(shape, jnp.bfloat16) for shape in shapes]
        + [
            pltpu.VMEM((rows, depth), jnp.bfloat16),
            pltpu.VMEM((blocks, depth, width), jnp.bfloat16),
            pltpu.SemaphoreType.DMA((count,)),
            pltpu.SemaphoreType.DMA((blocks,)),
            pltpu.SemaphoreType.DMA((len(parts), groups)),
        ],
        compiler_params=kernel_params(limit),
        cost_estimate=pl.CostEstimate(
            flops=2 * rows * depth * quarter * groups,
            bytes_accessed=2 * (weights.size + rows * depth + rows * quarter * groups),
            transcendentals=0,
        ),
        name="down_rows",
    )(place, hidden, weights, *after)


def add_kernel(count, later, part_ref, *refs):
    out_refs = refs[later : later + count]
    groups = part_ref.shape[1]
    for i, out_ref in enumerate(out_refs):
        for core in range(CORES):
            values = [part_ref[core, g, i].astype(jnp.float32) for g in range(groups)]
            out_ref[core] = functools.reduce(jnp.add, values).astype(jnp.bfloat16)


def add_groups(parts, later=()):
    cores, groups, count, capacity, quarter = parts.shape
    anywhere = pl.BlockSpec(memory_space=pl.ANY)
    whole = pl.BlockSpec(memory_space=pltpu.VMEM)
    out = pl.pallas_call(
        functools.partial(add_kernel, count, len(later)),
        in_specs=[whole] + [anywhere] * len(later),
        out_specs=[whole] * count + [anywhere] * len(later),
        out_shape=[jax.ShapeDtypeStruct((cores, capacity, quarter), jnp.bfloat16)] * count
        + [jax.ShapeDtypeStruct(v.shape, v.dtype) for v in later],
        input_output_aliases={1 + i: count + i for i in range(len(later))},
        compiler_params=kernel_params(),
        cost_estimate=pl.CostEstimate(
            flops=parts.size, bytes_accessed=3 * parts.size, transcendentals=0
        ),
        name="add_groups",
    )(parts, *later)
    return out[:count], out[count:]


def picked(table, piece_refs):
    rows = jnp.concatenate(
        [r[core].astype(jnp.float32) for r in piece_refs for core in range(CORES)], axis=0
    )
    rows = rows.astype(jnp.bfloat16)
    high_ref, low_ref = table
    return jnp.dot(high_ref[...], rows, preferred_element_type=jnp.float32) + jnp.dot(
        low_ref[...], rows, preferred_element_type=jnp.float32
    )


def combine_first_kernel(high_ref, low_ref, residual_ref, *refs):
    refs[-1][...] = picked((high_ref, low_ref), refs[:-1]) + residual_ref[...].astype(jnp.float32)


def combine_first(table, residual, pieces):
    return pl.pallas_call(
        combine_first_kernel,
        out_shape=jax.ShapeDtypeStruct(residual.shape, jnp.float32),
        compiler_params=kernel_params(),
        cost_estimate=pl.CostEstimate(
            flops=FIRST_FLOPS, bytes_accessed=8 * residual.size, transcendentals=0
        ),
        name="combine_first",
    )(*table, residual, *pieces)


def combine_last_kernel(high_ref, low_ref, begun_ref, *refs):
    piece_refs, (stream_ref, square_ref) = refs[:-2], refs[-2:]
    stream = begun_ref[...] + picked((high_ref, low_ref), piece_refs)
    stream_ref[...] = stream
    square = stream * stream
    lanes = stream.shape[0]
    folded = functools.reduce(
        jnp.add, [square[:, i : i + lanes] for i in range(0, square.shape[1], lanes)]
    )
    square_ref[...] = jnp.sum(folded.T, axis=0, keepdims=True)


def combine_last(table, begun, pieces):
    return pl.pallas_call(
        combine_last_kernel,
        out_shape=(
            jax.ShapeDtypeStruct(begun.shape, jnp.float32),
            jax.ShapeDtypeStruct((1, begun.shape[0]), jnp.float32),
        ),
        compiler_params=kernel_params(),
        name="combine_last",
    )(*table, begun, *pieces)


def norm_kernel(width, stream_ref, square_ref, gain_ref, out_ref):
    lanes = stream_ref.shape[0]
    square_total = jnp.sum(square_ref[...], axis=0, keepdims=True)
    inverse = lax.rsqrt(square_total / width + EPSILON)
    inverse = jnp.broadcast_to(inverse, (lanes, lanes)).T
    for i in range(0, stream_ref.shape[1], lanes):
        out_ref[:, i : i + lanes] = (
            stream_ref[:, i : i + lanes] * inverse * gain_ref[:, i : i + lanes]
        ).astype(jnp.bfloat16)


def norm(stream, square_parts, gain, width):
    return pl.pallas_call(
        functools.partial(norm_kernel, width),
        out_shape=jax.ShapeDtypeStruct(stream.shape, jnp.bfloat16),
        compiler_params=kernel_params(),
        name="norm",
    )(stream, square_parts, gain)


def body(residual, expert_ids, gate_prob, expert_hidden, w_down, norm_gain):
    chips = lax.axis_size("chip")
    groups = lax.axis_size("tensor")
    capacity, depth = expert_hidden.shape[2:]
    model_width = w_down.shape[2]
    chip = lax.axis_index("chip")
    place = jnp.stack([chip]).astype(jnp.int32)

    def to_chip(value, shift):
        if not shift:
            return value
        return lax.ppermute(value, "chip", [(i, i ^ shift) for i in range(chips)])

    def keys_of(shifts):
        expert = jnp.stack(
            [(chip ^ s) * CORES + core for s in shifts for core in range(CORES)]
        )
        slot = jnp.arange(capacity, dtype=jnp.int32)
        return (expert[:, None] * KEY_STRIDE + slot[None, :]).reshape(1, -1)

    first, last = (2,), (3, 1, 0)
    table_first, table_last = routing_tables(
        expert_ids, gate_prob, [keys_of(first), keys_of(last)]
    )

    hidden = expert_hidden.reshape(chips, CORES * capacity, depth)
    weights = w_down[0]
    far, near, here = PARTS
    far_value, near_value = down(place, hidden, weights, (far, near), groups, DOWN_VMEM_LIMIT)

    def to_tokens(value, part, later=()):
        shape = value.shape
        value = lax.all_to_all(
            value.reshape(CORES * groups, *shape[2:]), ("core", "tensor"), 0, 0, tiled=True
        )
        summed, later = add_groups(value.reshape(shape), later)
        return summed, later, [(s, to_chip(v, s)) for v, s in zip(summed, part)]

    far_summed, _, far_pieces = to_tokens(far_value, far)
    here_value = down(place, hidden, weights, (here,), groups, HERE_VMEM_LIMIT, far_summed)
    _, (here_value,), near_pieces = to_tokens(near_value, near, here_value)
    _, _, here_pieces = to_tokens(here_value, here)
    pieces = dict(far_pieces + near_pieces + here_pieces)
    begun = combine_first(table_first, residual, [pieces[s] for s in first])
    stream, squares = combine_last(table_last, begun, [pieces[s] for s in last])
    square_parts = lax.all_gather(squares, "tensor", axis=0, tiled=True)
    return norm(stream, square_parts, norm_gain[None, :], model_width)


def solution(mesh):
    dp, expert, tensor = mesh.devices.shape
    cores = Mesh(
        mesh.devices.reshape(dp, expert // CORES, CORES, tensor), ("dp", "chip", "core", "tensor")
    )
    tokens = ("dp", "chip", "core")
    placed = (
        P(tokens, "tensor"),
        P(tokens, None),
        P(tokens, None),
        P(("chip", "core"), "dp", None, "tensor"),
        P(("chip", "core"), "tensor", None),
        P("tensor"),
    )
    return jax.shard_map(
        body, mesh=cores, in_specs=placed, out_specs=P(tokens, "tensor"), check_vma=False
    )
```

```python
import functools

import jax
import jax.numpy as jnp
from jax import lax
from jax.experimental import pallas as pl
from jax.experimental.pallas import tpu as pltpu
from jax.sharding import Mesh
from jax.sharding import PartitionSpec as P

EXPERTS = 16
KEY_STRIDE = 64
EPSILON = 1e-05
VMEM_LIMIT = 32 * 1024 * 1024
DOWN_VMEM_LIMIT = 60 * 1024 * 1024
HERE_VMEM_LIMIT = 48 * 1024 * 1024
CORES = 2
FIRST_FLOPS = 40_000_000_000
W_BLOCK = 512
AHEAD = 3
PARTS = ((2,), (3, 1), (0,))


def kernel_params(limit=VMEM_LIMIT):
    return pltpu.CompilerParams(vmem_limit_bytes=limit)


def routing_kernel(ids_ref, gate_ref, *refs):
    tables = len(refs) // 3
    tokens, topk = ids_ref.shape
    ids = ids_ref[...]
    gate = gate_ref[...]
    lane = lax.broadcasted_iota(jnp.int32, (tokens, EXPERTS), 1)
    hits = [ids[:, k : k + 1] == lane for k in range(topk)]
    named = functools.reduce(jnp.add, [jnp.where(h, 1.0, 0.0) for h in hits])
    earlier = jnp.where(
        lax.broadcasted_iota(jnp.int32, (tokens, tokens), 1)
        < lax.broadcasted_iota(jnp.int32, (tokens, tokens), 0),
        1.0,
        0.0,
    )
    prefix = jnp.dot(
        earlier.astype(jnp.bfloat16),
        named.astype(jnp.bfloat16),
        preferred_element_type=jnp.float32,
    )
    positions = [
        jnp.sum(jnp.where(hits[k], prefix, 0.0), axis=1, keepdims=True) for k in range(topk)
    ]
    keys = [
        ids[:, k : k + 1] * KEY_STRIDE + positions[k].astype(jnp.int32) for k in range(topk)
    ]
    for key_ref, high_ref, low_ref in zip(refs[:tables], refs[tables::2], refs[tables + 1 :: 2]):
        key_of_slot = key_ref[...]
        table = jnp.zeros((tokens, key_ref.shape[1]), jnp.float32)
        for k in range(topk):
            table = table + jnp.where(keys[k] == key_of_slot, gate[:, k : k + 1], 0.0)
        high = table.astype(jnp.bfloat16)
        high_ref[...] = high
        low_ref[...] = (table - high.astype(jnp.float32)).astype(jnp.bfloat16)


def routing_tables(ids, gate, keys):
    out = pl.pallas_call(
        routing_kernel,
        out_shape=[
            jax.ShapeDtypeStruct((ids.shape[0], key.shape[1]), jnp.bfloat16)
            for key in keys
            for _ in range(2)
        ],
        compiler_params=kernel_params(),
        name="routing_tables",
    )(ids, gate, *keys)
    return list(zip(out[0::2], out[1::2]))


def down_kernel(parts, place_ref, hidden_ref, w_ref, *refs):
    refs = refs[len(refs) - 2 * len(parts) - 5 :]
    out_refs, refs = refs[: len(parts)], refs[len(parts) :]
    held_refs, (rows_ref, w_held, rows_sem, w_sem, out_sem) = refs[: len(parts)], refs[len(parts) :]
    chips, height, _ = hidden_ref.shape
    blocks, _, width = w_held.shape
    _, groups, _, capacity, quarter = out_refs[0].shape
    shifts = [s for part in parts for s in part]
    row_copies = [
        pltpu.make_async_copy(
            hidden_ref.at[jnp.bitwise_xor(place_ref[0], s)],
            rows_ref.at[i * height : (i + 1) * height],
            rows_sem.at[i],
        )
        for i, s in enumerate(shifts)
    ]
    w_copies = [
        pltpu.make_async_copy(
            w_ref.at[:, n * width : (n + 1) * width], w_held.at[n], w_sem.at[n]
        )
        for n in range(blocks)
    ]
    out_copies = [
        [
            pltpu.make_async_copy(held.at[:, g], out.at[:, g], out_sem.at[i, g])
            for i, (held, out) in enumerate(zip(held_refs, out_refs))
        ]
        for g in range(groups)
    ]
    for copy in row_copies + w_copies[:AHEAD]:
        copy.start()
    for copy in row_copies:
        copy.wait()
    stored = 0
    for n in range(blocks):
        w_copies[n].wait()
        if n + AHEAD < blocks:
            w_copies[n + AHEAD].start()
        value = jnp.dot(rows_ref[...], w_held[n], preferred_element_type=jnp.float32)
        begin, end = n * width, (n + 1) * width
        left = begin
        while left < end:
            g = left // quarter
            right = min(end, (g + 1) * quarter)
            first = 0
            for part, held in zip(parts, held_refs):
                for i in range(len(part)):
                    for core in range(CORES):
                        held[core, g, i, :, left - g * quarter : right - g * quarter] = value[
                            first : first + capacity, left - begin : right - begin
                        ].astype(jnp.bfloat16)
                        first += capacity
            left = right
        while (stored + 1) * quarter <= end:
            for copy in out_copies[stored]:
                copy.start()
            stored += 1
    for copies in out_copies:
        for copy in copies:
            copy.wait()


def down(place, hidden, weights, parts, groups, limit, after=()):
    chips, height, depth = hidden.shape
    width = W_BLOCK
    quarter = weights.shape[1] // groups
    capacity = height // CORES
    blocks = weights.shape[1] // width
    shapes = [(CORES, groups, len(part), capacity, quarter) for part in parts]
    count = sum(map(len, parts))
    rows = count * height
    anywhere = pl.BlockSpec(memory_space=pl.ANY)
    return pl.pallas_call(
        functools.partial(down_kernel, parts),
        in_specs=[pl.BlockSpec(memory_space=pltpu.SMEM)] + [anywhere] * (2 + len(after)),
        out_specs=[anywhere] * len(parts),
        out_shape=[jax.ShapeDtypeStruct(shape, jnp.bfloat16) for shape in shapes],
        scratch_shapes=[pltpu.VMEM(shape, jnp.bfloat16) for shape in shapes]
        + [
            pltpu.VMEM((rows, depth), jnp.bfloat16),
            pltpu.VMEM((blocks, depth, width), jnp.bfloat16),
            pltpu.SemaphoreType.DMA((count,)),
            pltpu.SemaphoreType.DMA((blocks,)),
            pltpu.SemaphoreType.DMA((len(parts), groups)),
        ],
        compiler_params=kernel_params(limit),
        cost_estimate=pl.CostEstimate(
            flops=2 * rows * depth * quarter * groups,
            bytes_accessed=2 * (weights.size + rows * depth + rows * quarter * groups),
            transcendentals=0,
        ),
        name="down_rows",
    )(place, hidden, weights, *after)


def add_kernel(count, later, part_ref, *refs):
    out_refs = refs[later : later + count]
    groups = part_ref.shape[1]
    for i, out_ref in enumerate(out_refs):
        for core in range(CORES):
            values = [part_ref[core, g, i].astype(jnp.float32) for g in range(groups)]
            out_ref[core] = functools.reduce(jnp.add, values).astype(jnp.bfloat16)


def add_groups(parts, later=()):
    cores, groups, count, capacity, quarter = parts.shape
    anywhere = pl.BlockSpec(memory_space=pl.ANY)
    whole = pl.BlockSpec(memory_space=pltpu.VMEM)
    out = pl.pallas_call(
        functools.partial(add_kernel, count, len(later)),
        in_specs=[whole] + [anywhere] * len(later),
        out_specs=[whole] * count + [anywhere] * len(later),
        out_shape=[jax.ShapeDtypeStruct((cores, capacity, quarter), jnp.bfloat16)] * count
        + [jax.ShapeDtypeStruct(v.shape, v.dtype) for v in later],
        input_output_aliases={1 + i: count + i for i in range(len(later))},
        compiler_params=kernel_params(),
        cost_estimate=pl.CostEstimate(
            flops=parts.size, bytes_accessed=3 * parts.size, transcendentals=0
        ),
        name="add_groups",
    )(parts, *later)
    return out[:count], out[count:]


def picked(table, piece_refs):
    rows = jnp.concatenate(
        [r[core].astype(jnp.float32) for r in piece_refs for core in range(CORES)], axis=0
    )
    rows = rows.astype(jnp.bfloat16)
    high_ref, low_ref = table
    return jnp.dot(high_ref[...], rows, preferred_element_type=jnp.float32) + jnp.dot(
        low_ref[...], rows, preferred_element_type=jnp.float32
    )


def combine_first_kernel(high_ref, low_ref, residual_ref, *refs):
    refs[-1][...] = picked((high_ref, low_ref), refs[:-1]) + residual_ref[...].astype(jnp.float32)


def combine_first(table, residual, pieces):
    return pl.pallas_call(
        combine_first_kernel,
        out_shape=jax.ShapeDtypeStruct(residual.shape, jnp.float32),
        compiler_params=kernel_params(),
        cost_estimate=pl.CostEstimate(
            flops=FIRST_FLOPS, bytes_accessed=8 * residual.size, transcendentals=0
        ),
        name="combine_first",
    )(*table, residual, *pieces)


def combine_last_kernel(high_ref, low_ref, begun_ref, *refs):
    piece_refs, (stream_ref, square_ref) = refs[:-2], refs[-2:]
    stream = begun_ref[...] + picked((high_ref, low_ref), piece_refs)
    stream_ref[...] = stream
    square = stream * stream
    lanes = stream.shape[0]
    folded = functools.reduce(
        jnp.add, [square[:, i : i + lanes] for i in range(0, square.shape[1], lanes)]
    )
    square_ref[...] = jnp.sum(folded.T, axis=0, keepdims=True)


def combine_last(table, begun, pieces):
    return pl.pallas_call(
        combine_last_kernel,
        out_shape=(
            jax.ShapeDtypeStruct(begun.shape, jnp.float32),
            jax.ShapeDtypeStruct((1, begun.shape[0]), jnp.float32),
        ),
        compiler_params=kernel_params(),
        name="combine_last",
    )(*table, begun, *pieces)


def norm_kernel(width, stream_ref, square_ref, gain_ref, out_ref):
    lanes = stream_ref.shape[0]
    square_total = jnp.sum(square_ref[...], axis=0, keepdims=True)
    inverse = lax.rsqrt(square_total / width + EPSILON)
    inverse = jnp.broadcast_to(inverse, (lanes, lanes)).T
    for i in range(0, stream_ref.shape[1], lanes):
        out_ref[:, i : i + lanes] = (
            stream_ref[:, i : i + lanes] * inverse * gain_ref[:, i : i + lanes]
        ).astype(jnp.bfloat16)


def norm(stream, square_parts, gain, width):
    return pl.pallas_call(
        functools.partial(norm_kernel, width),
        out_shape=jax.ShapeDtypeStruct(stream.shape, jnp.bfloat16),
        compiler_params=kernel_params(),
        name="norm",
    )(stream, square_parts, gain)


def body(residual, expert_ids, gate_prob, expert_hidden, w_down, norm_gain):
    chips = lax.axis_size("chip")
    groups = lax.axis_size("tensor")
    capacity, depth = expert_hidden.shape[2:]
    model_width = w_down.shape[2]
    chip = lax.axis_index("chip")
    place = jnp.stack([chip]).astype(jnp.int32)

    def to_chip(value, shift):
        if not shift:
            return value
        return lax.ppermute(value, "chip", [(i, i ^ shift) for i in range(chips)])

    def keys_of(shifts):
        expert = jnp.stack(
            [(chip ^ s) * CORES + core for s in shifts for core in range(CORES)]
        )
        slot = jnp.arange(capacity, dtype=jnp.int32)
        return (expert[:, None] * KEY_STRIDE + slot[None, :]).reshape(1, -1)

    first, last = (2,), (3, 1, 0)
    table_first, table_last = routing_tables(
        expert_ids, gate_prob, [keys_of(first), keys_of(last)]
    )

    hidden = expert_hidden.reshape(chips, CORES * capacity, depth)
    weights = w_down[0]
    far, near, here = PARTS
    (far_value,) = down(place, hidden, weights, (far,), groups, DOWN_VMEM_LIMIT)
    (near_value,) = down(place, hidden, weights, (near,), groups, DOWN_VMEM_LIMIT)

    def to_tokens(value, part, later=()):
        shape = value.shape
        value = lax.all_to_all(
            value.reshape(CORES * groups, *shape[2:]), ("core", "tensor"), 0, 0, tiled=True
        )
        summed, later = add_groups(value.reshape(shape), later)
        return summed, later, [(s, to_chip(v, s)) for v, s in zip(summed, part)]

    far_summed, _, far_pieces = to_tokens(far_value, far)
    here_value = down(place, hidden, weights, (here,), groups, HERE_VMEM_LIMIT, far_summed)
    _, (here_value,), near_pieces = to_tokens(near_value, near, here_value)
    _, _, here_pieces = to_tokens(here_value, here)
    pieces = dict(far_pieces + near_pieces + here_pieces)
    begun = combine_first(table_first, residual, [pieces[s] for s in first])
    stream, squares = combine_last(table_last, begun, [pieces[s] for s in last])
    square_parts = lax.all_gather(squares, "tensor", axis=0, tiled=True)
    return norm(stream, square_parts, norm_gain[None, :], model_width)


def solution(mesh):
    dp, expert, tensor = mesh.devices.shape
    cores = Mesh(
        mesh.devices.reshape(dp, expert // CORES, CORES, tensor), ("dp", "chip", "core", "tensor")
    )
    tokens = ("dp", "chip", "core")
    placed = (
        P(tokens, "tensor"),
        P(tokens, None),
        P(tokens, None),
        P(("chip", "core"), "dp", None, "tensor"),
        P(("chip", "core"), "tensor", None),
        P("tensor"),
    )
    return jax.shard_map(
        body, mesh=cores, in_specs=placed, out_specs=P(tokens, "tensor"), check_vma=False
    )
```

```python
import functools

import jax
import jax.numpy as jnp
from jax import lax
from jax.experimental import pallas as pl
from jax.experimental.pallas import tpu as pltpu
from jax.sharding import Mesh
from jax.sharding import PartitionSpec as P

EXPERTS = 16
KEY_STRIDE = 64
EPSILON = 1e-05
VMEM_LIMIT = 32 * 1024 * 1024
DOWN_VMEM_LIMIT = 60 * 1024 * 1024
HERE_VMEM_LIMIT = 48 * 1024 * 1024
CORES = 2
FIRST_FLOPS = 40_000_000_000
W_BLOCK = 512
AHEAD = 3
PARTS = ((2,), (3, 1), (0,))


def kernel_params(limit=VMEM_LIMIT):
    return pltpu.CompilerParams(vmem_limit_bytes=limit)


def routing_kernel(ids_ref, gate_ref, *refs):
    tables = len(refs) // 3
    tokens, topk = ids_ref.shape
    ids = ids_ref[...]
    gate = gate_ref[...]
    lane = lax.broadcasted_iota(jnp.int32, (tokens, EXPERTS), 1)
    hits = [ids[:, k : k + 1] == lane for k in range(topk)]
    named = functools.reduce(jnp.add, [jnp.where(h, 1.0, 0.0) for h in hits])
    earlier = jnp.where(
        lax.broadcasted_iota(jnp.int32, (tokens, tokens), 1)
        < lax.broadcasted_iota(jnp.int32, (tokens, tokens), 0),
        1.0,
        0.0,
    )
    prefix = jnp.dot(
        earlier.astype(jnp.bfloat16),
        named.astype(jnp.bfloat16),
        preferred_element_type=jnp.float32,
    )
    positions = [
        jnp.sum(jnp.where(hits[k], prefix, 0.0), axis=1, keepdims=True) for k in range(topk)
    ]
    keys = [
        ids[:, k : k + 1] * KEY_STRIDE + positions[k].astype(jnp.int32) for k in range(topk)
    ]
    for key_ref, high_ref, low_ref in zip(refs[:tables], refs[tables::2], refs[tables + 1 :: 2]):
        key_of_slot = key_ref[...]
        table = jnp.zeros((tokens, key_ref.shape[1]), jnp.float32)
        for k in range(topk):
            table = table + jnp.where(keys[k] == key_of_slot, gate[:, k : k + 1], 0.0)
        high = table.astype(jnp.bfloat16)
        high_ref[...] = high
        low_ref[...] = (table - high.astype(jnp.float32)).astype(jnp.bfloat16)


def routing_tables(ids, gate, keys):
    out = pl.pallas_call(
        routing_kernel,
        out_shape=[
            jax.ShapeDtypeStruct((ids.shape[0], key.shape[1]), jnp.bfloat16)
            for key in keys
            for _ in range(2)
        ],
        compiler_params=kernel_params(),
        name="routing_tables",
    )(ids, gate, *keys)
    return list(zip(out[0::2], out[1::2]))


def down_kernel(parts, place_ref, hidden_ref, w_ref, *refs):
    refs = refs[len(refs) - 2 * len(parts) - 5 :]
    out_refs, refs = refs[: len(parts)], refs[len(parts) :]
    held_refs, (rows_ref, w_held, rows_sem, w_sem, out_sem) = refs[: len(parts)], refs[len(parts) :]
    chips, height, _ = hidden_ref.shape
    blocks, _, width = w_held.shape
    _, groups, _, capacity, quarter = out_refs[0].shape
    shifts = [s for part in parts for s in part]
    row_copies = [
        pltpu.make_async_copy(
            hidden_ref.at[jnp.bitwise_xor(place_ref[0], s)],
            rows_ref.at[i * height : (i + 1) * height],
            rows_sem.at[i],
        )
        for i, s in enumerate(shifts)
    ]
    w_copies = [
        pltpu.make_async_copy(
            w_ref.at[:, n * width : (n + 1) * width], w_held.at[n], w_sem.at[n]
        )
        for n in range(blocks)
    ]
    out_copies = [
        [
            pltpu.make_async_copy(held.at[:, g], out.at[:, g], out_sem.at[i, g])
            for i, (held, out) in enumerate(zip(held_refs, out_refs))
        ]
        for g in range(groups)
    ]
    for copy in row_copies + w_copies[:AHEAD]:
        copy.start()
    for copy in row_copies:
        copy.wait()
    stored = 0
    for n in range(blocks):
        w_copies[n].wait()
        if n + AHEAD < blocks:
            w_copies[n + AHEAD].start()
        value = jnp.dot(rows_ref[...], w_held[n], preferred_element_type=jnp.float32)
        begin, end = n * width, (n + 1) * width
        left = begin
        while left < end:
            g = left // quarter
            right = min(end, (g + 1) * quarter)
            first = 0
            for part, held in zip(parts, held_refs):
                for i in range(len(part)):
                    for core in range(CORES):
                        held[core, g, i, :, left - g * quarter : right - g * quarter] = value[
                            first : first + capacity, left - begin : right - begin
                        ].astype(jnp.bfloat16)
                        first += capacity
            left = right
        while (stored + 1) * quarter <= end:
            for copy in out_copies[stored]:
                copy.start()
            stored += 1
    for copies in out_copies:
        for copy in copies:
            copy.wait()


def down(place, hidden, weights, parts, groups, limit, after=()):
    chips, height, depth = hidden.shape
    width = W_BLOCK
    quarter = weights.shape[1] // groups
    capacity = height // CORES
    blocks = weights.shape[1] // width
    shapes = [(CORES, groups, len(part), capacity, quarter) for part in parts]
    count = sum(map(len, parts))
    rows = count * height
    anywhere = pl.BlockSpec(memory_space=pl.ANY)
    return pl.pallas_call(
        functools.partial(down_kernel, parts),
        in_specs=[pl.BlockSpec(memory_space=pltpu.SMEM)] + [anywhere] * (2 + len(after)),
        out_specs=[anywhere] * len(parts),
        out_shape=[jax.ShapeDtypeStruct(shape, jnp.bfloat16) for shape in shapes],
        scratch_shapes=[pltpu.VMEM(shape, jnp.bfloat16) for shape in shapes]
        + [
            pltpu.VMEM((rows, depth), jnp.bfloat16),
            pltpu.VMEM((blocks, depth, width), jnp.bfloat16),
            pltpu.SemaphoreType.DMA((count,)),
            pltpu.SemaphoreType.DMA((blocks,)),
            pltpu.SemaphoreType.DMA((len(parts), groups)),
        ],
        compiler_params=kernel_params(limit),
        cost_estimate=pl.CostEstimate(
            flops=2 * rows * depth * quarter * groups,
            bytes_accessed=2 * (weights.size + rows * depth + rows * quarter * groups),
            transcendentals=0,
        ),
        name="down_rows",
    )(place, hidden, weights, *after)


def add_kernel(count, later, part_ref, *refs):
    out_refs = refs[later : later + count]
    groups = part_ref.shape[1]
    for i, out_ref in enumerate(out_refs):
        for core in range(CORES):
            values = [part_ref[core, g, i].astype(jnp.float32) for g in range(groups)]
            out_ref[core] = functools.reduce(jnp.add, values).astype(jnp.bfloat16)


def add_groups(parts, later=()):
    cores, groups, count, capacity, quarter = parts.shape
    anywhere = pl.BlockSpec(memory_space=pl.ANY)
    whole = pl.BlockSpec(memory_space=pltpu.VMEM)
    out = pl.pallas_call(
        functools.partial(add_kernel, count, len(later)),
        in_specs=[whole] + [anywhere] * len(later),
        out_specs=[whole] * count + [anywhere] * len(later),
        out_shape=[jax.ShapeDtypeStruct((cores, capacity, quarter), jnp.bfloat16)] * count
        + [jax.ShapeDtypeStruct(v.shape, v.dtype) for v in later],
        input_output_aliases={1 + i: count + i for i in range(len(later))},
        compiler_params=kernel_params(),
        cost_estimate=pl.CostEstimate(
            flops=parts.size, bytes_accessed=3 * parts.size, transcendentals=0
        ),
        name="add_groups",
    )(parts, *later)
    return out[:count], out[count:]


def picked(table, piece_refs):
    rows = jnp.concatenate(
        [r[core].astype(jnp.float32) for r in piece_refs for core in range(CORES)], axis=0
    )
    rows = rows.astype(jnp.bfloat16)
    high_ref, low_ref = table
    return jnp.dot(high_ref[...], rows, preferred_element_type=jnp.float32) + jnp.dot(
        low_ref[...], rows, preferred_element_type=jnp.float32
    )


def combine_first_kernel(high_ref, low_ref, residual_ref, *refs):
    refs[-1][...] = picked((high_ref, low_ref), refs[:-1]) + residual_ref[...].astype(jnp.float32)


def combine_first(table, residual, pieces):
    return pl.pallas_call(
        combine_first_kernel,
        out_shape=jax.ShapeDtypeStruct(residual.shape, jnp.float32),
        compiler_params=kernel_params(),
        cost_estimate=pl.CostEstimate(
            flops=FIRST_FLOPS, bytes_accessed=8 * residual.size, transcendentals=0
        ),
        name="combine_first",
    )(*table, residual, *pieces)


def combine_last_kernel(high_ref, low_ref, begun_ref, *refs):
    piece_refs, (stream_ref, square_ref) = refs[:-2], refs[-2:]
    stream = begun_ref[...] + picked((high_ref, low_ref), piece_refs)
    stream_ref[...] = stream
    square = stream * stream
    lanes = stream.shape[0]
    folded = functools.reduce(
        jnp.add, [square[:, i : i + lanes] for i in range(0, square.shape[1], lanes)]
    )
    square_ref[...] = jnp.sum(folded.T, axis=0, keepdims=True)


def combine_last(table, begun, pieces):
    return pl.pallas_call(
        combine_last_kernel,
        out_shape=(
            jax.ShapeDtypeStruct(begun.shape, jnp.float32),
            jax.ShapeDtypeStruct((1, begun.shape[0]), jnp.float32),
        ),
        compiler_params=kernel_params(),
        name="combine_last",
    )(*table, begun, *pieces)


def norm_kernel(width, stream_ref, square_ref, gain_ref, out_ref):
    lanes = stream_ref.shape[0]
    square_total = jnp.sum(square_ref[...], axis=0, keepdims=True)
    inverse = lax.rsqrt(square_total / width + EPSILON)
    inverse = jnp.broadcast_to(inverse, (lanes, lanes)).T
    for i in range(0, stream_ref.shape[1], lanes):
        out_ref[:, i : i + lanes] = (
            stream_ref[:, i : i + lanes] * inverse * gain_ref[:, i : i + lanes]
        ).astype(jnp.bfloat16)


def norm(stream, square_parts, gain, width):
    return pl.pallas_call(
        functools.partial(norm_kernel, width),
        out_shape=jax.ShapeDtypeStruct(stream.shape, jnp.bfloat16),
        compiler_params=kernel_params(),
        name="norm",
    )(stream, square_parts, gain)


def body(residual, expert_ids, gate_prob, expert_hidden, w_down, norm_gain):
    chips = lax.axis_size("chip")
    groups = lax.axis_size("tensor")
    capacity, depth = expert_hidden.shape[2:]
    model_width = w_down.shape[2]
    chip = lax.axis_index("chip")
    place = jnp.stack([chip]).astype(jnp.int32)

    def to_chip(value, shift):
        if not shift:
            return value
        return lax.ppermute(value, "chip", [(i, i ^ shift) for i in range(chips)])

    def keys_of(shifts):
        expert = jnp.stack(
            [(chip ^ s) * CORES + core for s in shifts for core in range(CORES)]
        )
        slot = jnp.arange(capacity, dtype=jnp.int32)
        return (expert[:, None] * KEY_STRIDE + slot[None, :]).reshape(1, -1)

    first, last = (2,), (3, 1, 0)
    table_first, table_last = routing_tables(
        expert_ids, gate_prob, [keys_of(first), keys_of(last)]
    )

    hidden = expert_hidden.reshape(chips, CORES * capacity, depth)
    weights = w_down[0]
    far, near, here = PARTS
    (far_value,) = down(place, hidden, weights, (far,), groups, DOWN_VMEM_LIMIT)
    (near_value,) = down(
        place, hidden, weights, (near,), groups, DOWN_VMEM_LIMIT, table_first[:1]
    )

    def to_tokens(value, part, later=()):
        shape = value.shape
        value = lax.all_to_all(
            value.reshape(CORES * groups, *shape[2:]), ("core", "tensor"), 0, 0, tiled=True
        )
        summed, later = add_groups(value.reshape(shape), later)
        return summed, later, [(s, to_chip(v, s)) for v, s in zip(summed, part)]

    far_summed, _, far_pieces = to_tokens(far_value, far)
    here_value = down(place, hidden, weights, (here,), groups, HERE_VMEM_LIMIT, far_summed)
    _, (here_value,), near_pieces = to_tokens(near_value, near, here_value)
    _, _, here_pieces = to_tokens(here_value, here)
    pieces = dict(far_pieces + near_pieces + here_pieces)
    begun = combine_first(table_first, residual, [pieces[s] for s in first])
    stream, squares = combine_last(table_last, begun, [pieces[s] for s in last])
    square_parts = lax.all_gather(squares, "tensor", axis=0, tiled=True)
    return norm(stream, square_parts, norm_gain[None, :], model_width)


def solution(mesh):
    dp, expert, tensor = mesh.devices.shape
    cores = Mesh(
        mesh.devices.reshape(dp, expert // CORES, CORES, tensor), ("dp", "chip", "core", "tensor")
    )
    tokens = ("dp", "chip", "core")
    placed = (
        P(tokens, "tensor"),
        P(tokens, None),
        P(tokens, None),
        P(("chip", "core"), "dp", None, "tensor"),
        P(("chip", "core"), "tensor", None),
        P("tensor"),
    )
    return jax.shard_map(
        body, mesh=cores, in_specs=placed, out_specs=P(tokens, "tensor"), check_vma=False
    )
```
